32 devices in a mesh: ctx: 16 (over z, x, core), tp: 2 (over y).
Axes of the slice: x: 2, y: 2, z: 4, core: 2. Of those that a mesh axis runs over, the one named last changes fastest.
Arguments:
- queries: bfloat16 [2048, 4096], P('ctx', 'tp'), may hold values from -5 to 5
- keys: bfloat16 [2048, 1024], P('ctx', 'tp'), may hold values from -5 to 5
- values: bfloat16 [2048, 1024], P('ctx', 'tp'), may hold values from -6 to 6
- out_grad: bfloat16 [2048, 4096], P('ctx', 'tp'), may hold values from -6 to 6
- features: bfloat16 [2048, 4096], P('ctx'), may hold values from -6 to 6
- segment_ids: int32 [2048], replicated, may hold values from 0 to 15, never falling along the last dimension, each value on 1 to 1536 neighbouring positions
Outputs:
- query_grads: bfloat16 [2048, 4096], P('ctx', 'tp')
- weight_grad: float32 [4096, 1024], P('tp')
The draws below stay inside these ranges and needn't reach their ends.
Inputs may be any that keep to these rules, and one draw needn't show every extreme that they name: `segment_ids`: never falling along the sequence; each document has 1 to 1536 tokens and one has exactly 1536.
All inputs are finite; a program needn't handle non-finite values.
Results may differ from the reference program's by a relative error of at most 0.024.
Values may be sent and summed in bfloat16 or wider, within the bound.
A program may use at most 64 MiB of HBM per device.

```python
import math
import jax
import jax.numpy as jnp
import numpy as np
from jax import lax

QH = 32
KVH = 8
HD = 128
DX = 4096
SEGS = 16
TOKENS = 2048
MOST = 1536


def draw_queries(key, part):
    key = jax.random.fold_in(key, 3)
    return jnp.clip(1.6 * jax.random.normal(key, (TOKENS, QH * HD), jnp.float32), -5.0, 5.0).astype(jnp.bfloat16)


def draw_keys(key, part):
    key = jax.random.fold_in(key, 4)
    return jnp.clip(1.6 * jax.random.normal(key, (TOKENS, KVH * HD), jnp.float32), -5.0, 5.0).astype(jnp.bfloat16)


def level_of(rng, extent, cuts, least, top_value):
    loudness, own = 1.0, jax.random.fold_in(rng, 6)
    for axis_at, parts in cuts:
        draws = jnp.exp(jax.random.uniform(jax.random.fold_in(own, axis_at), (parts,), jnp.float32, least / len(cuts), top_value / len(cuts)))
        loudness = loudness * jnp.repeat(draws, extent[axis_at] // parts).reshape([-1 if axis == axis_at else 1 for axis in range(len(extent))])
    return loudness


def length_profile(number_of, total, bound, lean):
    weights = [(1 << 20) // math.isqrt(rank ** lean) + 1 for rank in range(2, number_of + 1)]
    spare, counts = total - bound - (number_of - 1), [1] * (number_of - 1)
    while spare > 0:
        candidates = [i for i in range(number_of - 1) if counts[i] < bound]
        mass, budget = sum([weights[i] for i in candidates]), spare
        for i in candidates:
            addition = min(bound - counts[i], max(1, budget * weights[i] // mass), spare)
            counts[i] = counts[i] + addition
            spare = spare - addition
    return np.array([bound] + counts)


def ragged_sizes(rng, number_of, total, limit, lean):
    if number_of == 2:
        one = jax.random.randint(rng, (), max(1, total - limit), min(limit, total - 1) + 1)
        return jnp.stack([one, total - one])
    sizes = jnp.asarray(length_profile(number_of, total, limit, lean), jnp.int32)
    twos = (number_of - 1) // 2
    donor, receiver = sizes[1:1 + 2 * twos:2], sizes[2:2 + 2 * twos:2]
    slack = jnp.minimum(donor - 1, limit - receiver)
    moved = jax.random.randint(jax.random.fold_in(rng, 1), (twos,), 0, 1 << 20) % (slack + 1)
    sizes = sizes.at[1:1 + 2 * twos:2].set(donor - moved).at[2:2 + 2 * twos:2].set(receiver + moved)
    return sizes[jax.random.permutation(jax.random.fold_in(rng, 2), number_of)]


def scatter_about(stream_key, shape, scale, limit, cuts=(), held_as=jnp.bfloat16):
    result = jax.random.normal(stream_key, shape, jnp.float32) * scale
    if len(cuts) > 0:
        result = level_of(stream_key, shape, cuts, -0.22, 0.18) * result
    return jnp.clip(result, min=-limit, max=limit).astype(held_as)


def setup_inputs(seed: int = 0) -> dict:
    key_list = jax.random.split(jax.random.key(seed), 7)
    queries = draw_queries(jax.random.fold_in(key_list[6], 71), 0)
    keys = draw_keys(jax.random.fold_in(key_list[6], 71), 0)
    values = scatter_about(key_list[2], (TOKENS, KVH * HD), 1.0, 6.0, ((0, 16), (1, 2)))
    out_grad = scatter_about(key_list[3], (TOKENS, QH * HD), 1.0, 6.0, ((0, 16), (1, 2)))
    features = scatter_about(key_list[4], (TOKENS, DX), 1.0, 6.0, ((0, 16),))
    segment_ids = jnp.searchsorted(jnp.cumsum(ragged_sizes(key_list[5], SEGS, TOKENS, MOST, 2)), jnp.arange(TOKENS), side="right").astype(jnp.int32)
    return {"queries": queries, "keys": keys, "values": values, "out_grad": out_grad, "features": features, "segment_ids": segment_ids}


def reference(queries, keys, values, out_grad, features, segment_ids):
    group = QH // KVH
    scale = HD ** (-0.5)
    block = math.gcd(TOKENS, 256)
    query_heads = queries.astype(jnp.float32).reshape(TOKENS, KVH, group, HD)
    grad_heads = out_grad.astype(jnp.float32).reshape(TOKENS, KVH, group, HD)
    key_heads = keys.astype(jnp.float32).reshape(TOKENS, KVH, HD)
    value_heads = values.astype(jnp.float32).reshape(TOKENS, KVH, HD)
    positions = jnp.arange(TOKENS, dtype=jnp.int32)

    def step(value_sum, start):
        query_block = lax.dynamic_slice_in_dim(query_heads, start, block, 0)
        grad_block = lax.dynamic_slice_in_dim(grad_heads, start, block, 0)
        seg_block = lax.dynamic_slice_in_dim(segment_ids, start, block, 0)
        pos_block = start + jnp.arange(block, dtype=jnp.int32)
        allowed = (positions[None, :] <= pos_block[:, None]) & (segment_ids[None, :] == seg_block[:, None])
        scores = jnp.einsum('qngd,knd->ngqk', query_block, key_heads) * scale
        scores = jnp.where(allowed, scores, -1e+30)
        top = lax.optimization_barrier(jnp.max(scores, axis=-1))
        weights = jnp.where(allowed, jnp.exp(scores - top[..., None]), 0.0)
        total = lax.optimization_barrier(jnp.sum(weights, axis=-1))
        weights_b = weights.astype(jnp.bfloat16).astype(jnp.float32)
        attended = (jnp.einsum('ngqk,knd->ngqd', weights_b, value_heads) / total[..., None]).astype(jnp.bfloat16)
        log_total = top + jnp.log(total)
        delta = jnp.einsum('qngd,ngqd->ngq', grad_block, attended.astype(jnp.float32))
        probs = jnp.where(allowed, jnp.exp(scores - log_total[..., None]), 0.0)
        dprob = jnp.einsum('qngd,knd->ngqk', grad_block, value_heads)
        dscore = probs * (dprob - delta[..., None])
        dscore_b = dscore.astype(jnp.bfloat16).astype(jnp.float32)
        probs_b = probs.astype(jnp.bfloat16).astype(jnp.float32)
        query_grad = (jnp.einsum('ngqk,knd->qngd', dscore_b, key_heads) * scale).astype(jnp.bfloat16)
        value_part = jnp.einsum('ngqk,qngd->knd', probs_b, grad_block)
        return (value_sum + value_part, query_grad)
    starts = jnp.arange(TOKENS // block, dtype=jnp.int32) * block
    value_grad, query_blocks = lax.scan(step, jnp.zeros((TOKENS, KVH, HD), jnp.float32), starts)
    query_grads = query_blocks.reshape(TOKENS, QH * HD)
    value_b = value_grad.reshape(TOKENS, KVH * HD).astype(jnp.bfloat16)
    weight_grad = jnp.dot(features.T, value_b, preferred_element_type=jnp.float32) * (1.0 / math.sqrt(TOKENS))
    return (query_grads, weight_grad)
```

```python
import functools
import math

import jax
import jax.numpy as jnp
from jax import lax
from jax.experimental import pallas as pl
from jax.experimental.pallas import tpu as pltpu
from jax.sharding import PartitionSpec as P

HD = 128
MESH = pl.DeviceIdType.MESH
BF16 = jnp.bfloat16
F32 = jnp.float32


def attention_kernel(
    span_ref, q_ref, do_ref, k_ref, v_ref, start_ref, pos_ref, dq_ref, vg_ref, s_ref, dp_ref, *, group, width
):
    rows = q_ref.shape[0]
    wide = group * rows
    nt = (((1,), (1,)), ((), ()))
    tn = (((0,), (0,)), ((), ()))
    coef = HD ** (-0.5) * math.log2(math.e)
    lo, hi = span_ref[0], span_ref[1]
    qs = jnp.concatenate([q_ref[:, g * HD : (g + 1) * HD] for g in range(group)], axis=0)
    ds = jnp.concatenate([do_ref[:, g * HD : (g + 1) * HD] for g in range(group)], axis=0)
    start, pos = start_ref[...], pos_ref[...]
    vg_ref[...] = jnp.zeros_like(vg_ref)

    def first(j, top):
        at = pl.ds(pl.multiple_of(j * width, width), width)
        s = lax.dot_general(k_ref[at, :], qs, nt, preferred_element_type=F32)
        kpos = j * width + lax.broadcasted_iota(jnp.int32, (width, wide), 0)
        s = jnp.where((kpos >= start) & (kpos <= pos), s * coef, -1e30)
        s_ref[at, :] = s
        return jnp.maximum(top, jnp.max(s, axis=0, keepdims=True))

    top = lax.fori_loop(lo, hi, first, jnp.full((1, wide), -1e30, F32))

    def second(j, carry):
        total, dsum = carry
        at = pl.ds(pl.multiple_of(j * width, width), width)
        dp = lax.dot_general(v_ref[at, :], ds, nt, preferred_element_type=F32)
        w = jnp.exp2(s_ref[at, :] - top)
        s_ref[at, :] = w
        dp_ref[at, :] = dp
        return (
            total + jnp.sum(w, axis=0, keepdims=True),
            dsum + jnp.sum(w * dp, axis=0, keepdims=True),
        )

    zero = jnp.zeros((1, wide), F32)
    total, dsum = lax.fori_loop(lo, hi, second, (zero, zero))
    inv = 1.0 / total
    delta = dsum * inv

    def third(j, acc):
        at = pl.ds(pl.multiple_of(j * width, width), width)
        p = s_ref[at, :] * inv
        g = p * (dp_ref[at, :] - delta)
        vg_ref[at, :] = jnp.dot(p.astype(BF16), ds, preferred_element_type=F32).astype(BF16)
        return acc + lax.dot_general(k_ref[at, :], g.astype(BF16), tn, preferred_element_type=F32)

    acc = lax.fori_loop(lo, hi, third, jnp.zeros((HD, wide), F32))
    dq = (acc * HD ** (-0.5)).T.astype(BF16)
    for g in range(group):
        dq_ref[:, g * HD : (g + 1) * HD] = dq[g * rows : (g + 1) * rows, :]


def attention(queries, out_grad, key_all, value_all, segment_ids, first):
    rows = queries.shape[0]
    tokens = segment_ids.shape[0]
    heads_kv = key_all.shape[1] // HD
    group = queries.shape[1] // HD // heads_kv
    width = math.gcd(tokens, 256)
    seg_own = lax.dynamic_slice_in_dim(segment_ids, first, rows, 0)
    start = jnp.sum((segment_ids[:, None] < seg_own[None, :]).astype(jnp.int32), axis=0)
    pos = first + jnp.arange(rows, dtype=jnp.int32)
    span = jnp.stack([start[0] // width, (first + rows + width - 1) // width])
    wide = group * rows
    column = lambda n, *_: (0, n)
    whole = lambda n, *_: (0, 0)
    return pl.pallas_call(
        functools.partial(attention_kernel, group=group, width=width),
        out_shape=(
            jax.ShapeDtypeStruct(queries.shape, BF16),
            jax.ShapeDtypeStruct(key_all.shape, BF16),
        ),
        grid_spec=pltpu.PrefetchScalarGridSpec(
            num_scalar_prefetch=1,
            grid=(heads_kv,),
            in_specs=[
                pl.BlockSpec((rows, group * HD), column),
                pl.BlockSpec((rows, group * HD), column),
                pl.BlockSpec((tokens, HD), column),
                pl.BlockSpec((tokens, HD), column),
                pl.BlockSpec((1, wide), whole),
                pl.BlockSpec((1, wide), whole),
            ],
            out_specs=[
                pl.BlockSpec((rows, group * HD), column),
                pl.BlockSpec((tokens, HD), column),
            ],
            scratch_shapes=[pltpu.VMEM((tokens, wide), F32), pltpu.VMEM((tokens, wide), F32)],
        ),
        compiler_params=pltpu.CompilerParams(vmem_limit_bytes=48 << 20),
        cost_estimate=pl.CostEstimate(
            flops=8 * wide * tokens * HD * heads_kv,
            bytes_accessed=4 * (key_all.size + queries.size) * 2,
            transcendentals=wide * tokens * heads_kv,
        ),
        name="attention",
    )(
        span.astype(jnp.int32),
        queries,
        out_grad,
        key_all,
        value_all,
        jnp.tile(start, group)[None, :],
        jnp.tile(pos, group)[None, :],
    )


class Place:
    def __init__(self, n):
        self.A, self.B, self.C = n // 4, 2, 2
        self.me = lax.axis_index("ctx")
        self.a = self.me // (self.B * self.C)
        self.b = lax.rem(self.me // self.C, self.B)
        self.c = lax.rem(self.me, self.C)
        self.steps = sorted(range(1, self.A), key=lambda k: min(k, self.A - k))

    def at(self, da=0, db=0, dc=0):
        a = lax.rem(self.a + da + self.A, self.A)
        b = lax.rem(self.b + db + self.B, self.B)
        c = lax.rem(self.c + dc + self.C, self.C)
        return (a * self.B + b) * self.C + c


def greet(place, tp_peers=()):
    barrier = pltpu.get_barrier_semaphore()
    peers = [{"ctx": place.at(da=k)} for k in place.steps]
    peers += [{"ctx": place.at(db=1)}, {"ctx": place.at(dc=1)}]
    peers += [{"tp": p} for p in tp_peers]
    for peer in peers:
        pl.semaphore_signal(barrier, inc=1, device_id=peer, device_id_type=MESH)
    pl.semaphore_wait(barrier, len(peers))


class Gather:
    def __init__(self, place, src, out, send, recv):
        self.p, self.src, self.out, self.send, self.recv = place, src, out, send, recv
        self.sent = []

    def copy(self, src, slot, sem, target):
        return pltpu.make_async_remote_copy(
            src_ref=src,
            dst_ref=self.out.at[slot],
            send_sem=self.send.at[sem],
            recv_sem=self.recv.at[sem],
            device_id={"ctx": target},
            device_id_type=MESH,
        )

    def push(self, src, slot, sem, target):
        copy = self.copy(src, slot, sem, target)
        copy.start()
        self.sent.append(copy)

    def arrived(self, slot, sem):
        self.copy(self.out.at[slot], slot, sem, self.p.at(dc=1)).wait_recv()

    def begin(self):
        p = self.p
        for k in p.steps:
            self.push(self.src, p.me, k, p.at(da=k))
        self.push(self.src, p.me, p.A, p.at(db=1))
        self.push(self.src, p.me, 2 * p.A, p.at(dc=1))

    def along_a(self, k):
        p = self.p
        slot = p.at(da=-k)
        self.arrived(slot, k)
        self.push(self.out.at[slot], slot, p.A + k, p.at(db=1))
        self.push(self.out.at[slot], slot, 2 * p.A + k, p.at(dc=1))

    def along_b(self, k):
        p = self.p
        slot = p.at(da=-k, db=1)
        self.arrived(slot, p.A + k)
        self.push(self.out.at[slot], slot, 3 * p.A + k, p.at(dc=1))

    def finish(self):
        p = self.p
        for k in range(p.A):
            self.arrived(p.at(da=-k, dc=1), 2 * p.A + k)
            self.arrived(p.at(da=-k, db=1, dc=1), 3 * p.A + k)
        for copy in self.sent:
            copy.wait_send()


def run_gathers(gathers, begun=0):
    p = gathers[0].p
    for g in gathers[begun:]:
        g.begin()
    for k in p.steps:
        for g in gathers:
            g.along_a(k)
    for k in [0] + p.steps:
        for g in gathers:
            g.along_b(k)
    for g in gathers:
        g.finish()


def gather_kernel(n, count, *refs):
    srcs, outs = refs[:count], refs[count : 2 * count]
    send, recv, own = refs[2 * count :]
    place = Place(n)
    local = []
    for i in range(count):
        copy = pltpu.make_async_copy(srcs[i], outs[i].at[place.me], own.at[i])
        copy.start()
        local.append(copy)
    greet(place)
    run_gathers([Gather(place, srcs[i], outs[i], send.at[i], recv.at[i]) for i in range(count)])
    for copy in local:
        copy.wait()


def gather(arrays, n, collective_id):
    count = len(arrays)
    outs = pl.pallas_call(
        functools.partial(gather_kernel, n, count),
        out_shape=[jax.ShapeDtypeStruct((n,) + a.shape, a.dtype) for a in arrays],
        in_specs=[pl.BlockSpec(memory_space=pl.ANY)] * count,
        out_specs=[pl.BlockSpec(memory_space=pl.ANY)] * count,
        scratch_shapes=[
            pltpu.SemaphoreType.DMA((count, n)),
            pltpu.SemaphoreType.DMA((count, n)),
            pltpu.SemaphoreType.DMA((count,)),
        ],
        compiler_params=pltpu.CompilerParams(collective_id=collective_id, has_side_effects=True),
        name="gather%d" % collective_id,
    )(*arrays)
    return [o.reshape((n * a.shape[0],) + a.shape[1:]) for o, a in zip(outs, arrays)]


def reduce_kernel(n, parts, out, mine, one, sum_one, two, sum_two, three, send, recv, own):
    place = Place(n)
    A = place.A
    order = place.steps + [0]
    a_of = {k: lax.rem(place.a + k, A) for k in order}
    local = {}
    for k in order:
        local[k] = pltpu.make_async_copy(
            parts.at[a_of[k], :, place.c], mine.at[a_of[k]], own.at[k]
        )
        local[k].start()
    greet(place)

    def remote(src, dst, sem, target):
        return pltpu.make_async_remote_copy(
            src_ref=src,
            dst_ref=dst,
            send_sem=send.at[sem],
            recv_sem=recv.at[sem],
            device_id={"ctx": target},
            device_id_type=MESH,
        )

    sib, side = place.at(dc=1), place.at(db=1)
    started = []
    core, cross, line = {}, {}, {}
    for k in order:
        core[k] = remote(parts.at[a_of[k], :, 1 - place.c], one.at[a_of[k]], k, sib)
        core[k].start()
    for k in order:
        local[k].wait()
        core[k].wait_recv()
        at = a_of[k]
        sum_one[at] = (mine[at].astype(F32) + one[at].astype(F32)).astype(BF16)
        cross[k] = remote(sum_one.at[at, 1 - place.b], two.at[at], A + k, side)
        cross[k].start()
    for k in order:
        cross[k].wait_recv()
        at = a_of[k]
        sum_two[at] = (sum_one[at, place.b].astype(F32) + two[at].astype(F32)).astype(BF16)
        if k:
            line[k] = remote(sum_two.at[at], three.at[k], 2 * A + k, place.at(da=k))
            line[k].start()
    total = sum_two[place.a].astype(F32)
    for k in place.steps:
        line[k].wait_recv()
        total = total + three[k].astype(F32)
    out[...] = total.astype(BF16)
    for copies in (core, cross, line):
        for copy in copies.values():
            copy.wait_send()


def reduce(parts, n, collective_id):
    rows, cols = parts.shape[0] // n, parts.shape[1]
    A = n // 4
    block = lambda *lead: pltpu.VMEM(lead + (rows, cols), BF16)
    return pl.pallas_call(
        functools.partial(reduce_kernel, n),
        out_shape=jax.ShapeDtypeStruct((rows, cols), BF16),
        in_specs=[pl.BlockSpec(memory_space=pl.ANY)],
        out_specs=pl.BlockSpec(memory_space=pltpu.VMEM),
        scratch_shapes=[
            block(A, 2),
            block(A, 2),
            block(A, 2),
            block(A),
            block(A),
            block(A),
            pltpu.SemaphoreType.DMA((n,)),
            pltpu.SemaphoreType.DMA((n,)),
            pltpu.SemaphoreType.DMA((A,)),
        ],
        compiler_params=pltpu.CompilerParams(
            collective_id=collective_id, has_side_effects=True, vmem_limit_bytes=32 << 20
        ),
        name="reduce",
    )(parts.reshape(A, 2, 2, rows, cols))


def spread_kernel(n, tp, w, out, send, recv, own, tp_send, tp_recv):
    place = Place(n)
    t = lax.axis_index("tp")
    local = pltpu.make_async_copy(w.at[t], out.at[t, place.me], own)
    local.start()
    others = [lax.rem(t + k, tp) for k in range(1, tp)]
    greet(place, others)
    copies = []
    for k in range(1, tp):
        copy = pltpu.make_async_remote_copy(
            src_ref=w.at[others[k - 1]],
            dst_ref=out.at[t, place.me],
            send_sem=tp_send.at[k],
            recv_sem=tp_recv.at[k],
            device_id={"tp": others[k - 1]},
            device_id_type=MESH,
        )
        copy.start()
        copies.append(copy)
    gathers = [Gather(place, w.at[t], out.at[t], send.at[0], recv.at[0])]
    gathers[0].begin()
    for k in range(1, tp):
        source = lax.rem(t - k + tp, tp)
        copies[k - 1].wait_recv()
        more = Gather(place, out.at[source, place.me], out.at[source], send.at[k], recv.at[k])
        more.begin()
        gathers.append(more)
    run_gathers(gathers, len(gathers))
    for copy in copies:
        copy.wait_send()
    local.wait()


def spread(w, n, tp, collective_id):
    return pl.pallas_call(
        functools.partial(spread_kernel, n, tp),
        out_shape=jax.ShapeDtypeStruct((tp, n) + w.shape[1:], BF16),
        in_specs=[pl.BlockSpec(memory_space=pl.ANY)],
        out_specs=pl.BlockSpec(memory_space=pl.ANY),
        scratch_shapes=[
            pltpu.SemaphoreType.DMA((tp, n)),
            pltpu.SemaphoreType.DMA((tp, n)),
            pltpu.SemaphoreType.DMA,
            pltpu.SemaphoreType.DMA((tp,)),
            pltpu.SemaphoreType.DMA((tp,)),
        ],
        compiler_params=pltpu.CompilerParams(collective_id=collective_id, has_side_effects=True),
        name="spread",
    )(w)


def widen_kernel(w_ref, out_ref):
    slots, rows, cols = w_ref.shape[1:]
    for i in range(w_ref.shape[0]):
        for j in range(slots):
            out_ref[j * rows : (j + 1) * rows, i * cols : (i + 1) * cols] = w_ref[i, j].astype(F32)


def widen(w):
    tp, n, rows, cols = w.shape
    slots = 2
    return pl.pallas_call(
        widen_kernel,
        out_shape=jax.ShapeDtypeStruct((n * rows, tp * cols), F32),
        grid=(n // slots,),
        in_specs=[pl.BlockSpec((tp, slots, rows, cols), lambda i: (0, i, 0, 0))],
        out_specs=pl.BlockSpec((slots * rows, tp * cols), lambda i: (i, 0)),
        compiler_params=pltpu.CompilerParams(vmem_limit_bytes=32 << 20),
        name="widen",
    )(w)


def per_device(n, tp, queries, keys, values, out_grad, features, segment_ids):
    rows = queries.shape[0]
    tokens = segment_ids.shape[0]
    inputs = features.shape[1]
    first = lax.axis_index("ctx") * rows
    factor = 1.0 / math.sqrt(tokens)
    contract = (((0,), (0,)), ((), ()))
    block = inputs // (n * tp)
    if n % 4 == 0 and rows % 16 == 0 and inputs % (n * tp) == 0 and block % 16 == 0:
        key_all, value_all = gather([keys, values], n, 0)
        cut = features.reshape(rows, tp, n, block).transpose(2, 0, 1, 3)
        own = lax.all_to_all(cut, "ctx", split_axis=0, concat_axis=0, tiled=True)
        own = own.reshape(tokens, tp * block)
        query_grads, parts = attention(queries, out_grad, key_all, value_all, segment_ids, first)
        value_b = reduce(parts, n, 1)
        (value_full,) = gather([value_b], n, 2)
        w = lax.dot_general(own, value_full, contract, preferred_element_type=F32) * factor
        w = w.astype(BF16).reshape(tp, block, -1)
        return query_grads, widen(spread(w, n, tp, 3))
    key_all = lax.all_gather(keys, "ctx", axis=0, tiled=True)
    value_all = lax.all_gather(values, "ctx", axis=0, tiled=True)
    query_grads, parts = attention(queries, out_grad, key_all, value_all, segment_ids, first)
    value_b = lax.psum_scatter(parts.astype(F32), "ctx", scatter_dimension=0, tiled=True).astype(BF16)
    term = lax.dot_general(features, value_b, contract, preferred_element_type=F32)
    summed = lax.psum(term, "ctx")
    weight_grad = lax.all_to_all(
        summed.astype(BF16), "tp", split_axis=0, concat_axis=1, tiled=True
    ).astype(F32)
    return query_grads, weight_grad * factor


def solution(mesh):
    placed = (P("ctx", "tp"), P("ctx", "tp"), P("ctx", "tp"), P("ctx", "tp"), P("ctx", None), P())
    return jax.shard_map(
        functools.partial(per_device, mesh.shape["ctx"], mesh.shape["tp"]),
        mesh=mesh,
        in_specs=placed,
        out_specs=(P("ctx", "tp"), P("tp", None)),
        check_vma=False,
    )
```
